32 devices in a mesh: req: 4 (over y, x), patch: 8 (over z, core).
Axes of the slice: x: 2, y: 2, z: 4, core: 2. Of those that a mesh axis runs over, the one named last changes fastest.
Arguments:
- field: float32 [64, 16, 640], P(('req', 'patch')), parts along dimension 0
- stale_conv_in: bfloat16 [64, 16, 640], P(('req', 'patch')), parts along dimension 0, may hold values from -6 to 6
- stale_keys: bfloat16 [1024, 320], P(('req', 'patch')), parts along dimension 0, may hold values from -6 to 6
- stale_values: bfloat16 [1024, 320], P(('req', 'patch')), parts along dimension 0, may hold values from -6 to 6
- norm1_gain: float32 [640], replicated, may hold values from 0.25 to 1.75
- norm1_bias: float32 [640], replicated, may hold values from -3 to 3
- conv_weight: bfloat16 [3, 3, 640, 640], P(None, None, None, 'patch'), may hold values from -0.078125 to 0.078125
- conv_bias: float32 [640], replicated, may hold values from -3 to 3
- time_embed: float32 [8, 640], P('req'), parts along dimension 0, may hold values from -5 to 5
- norm2_gain: float32 [640], replicated, may hold values from 0.25 to 1.75
- norm2_bias: float32 [640], replicated, may hold values from -3 to 3
- w_query: bfloat16 [640, 320], replicated
- w_keyvalue: bfloat16 [640, 640], replicated, may hold values from -0.25 to 0.25
- w_out: bfloat16 [320, 640], replicated, may hold values from -0.3125 to 0.3125
Outputs:
- outputs: float32 [2, 64, 16, 640], P(None, ('req', 'patch')), parts along dimension 1
The draws below stay inside these ranges and needn't reach their ends.
There are 4 independent parts, one for each index of `req`. The reference program is written for one: setup_inputs(seed, part) draws one part's arguments, and reference() takes and returns one part's arrays. A program takes and returns all parts, laid end to end along the dimension named above; an argument that names none is the same for every part. Nothing has to cross between parts.
All inputs are finite; a program needn't handle non-finite values.
Results may differ from the reference program's by a relative error of at most 0.0047.
Values may be sent and summed in bfloat16 or wider, within the bound.
A program may use at most 64 MiB of HBM per device.

```python
import jax
import jax.numpy as jnp
from jax import lax

CHANNELS = 640
GROUPS = 32
HEADS = 5
HEAD_DIM = 64
COLS = 16
KEY_WIDTH = 320
HEIGHT = 16
TOKENS = 256
N_PATCH = 8


def draw_field(key, part):
    base = jax.random.normal(jax.random.fold_in(key, 11), (HEIGHT, COLS, CHANNELS), jnp.float32)
    rising = 1.0 + 2.0 * jnp.arange(HEIGHT, dtype=jnp.float32) / HEIGHT
    result = base * rising[:, None, None]
    return result.astype(jnp.float32)


def draw_w_query(key, part):
    base = jax.random.normal(jax.random.fold_in(key, 21), (CHANNELS, KEY_WIDTH), jnp.float32)
    return (base * CHANNELS ** (-0.5)).astype(jnp.bfloat16)


def block_levels(key, dims, shards, low, high):
    loudness = 1.0
    for position, shards_of in shards:
        draws = jax.random.uniform(jax.random.fold_in(jax.random.fold_in(key, 6), position), (shards_of,), jnp.float32, low / len(shards), high / len(shards))
        loudness = loudness * jnp.repeat(jnp.exp(draws), dims[position] // shards_of).reshape((-1,) + (1,) * (len(dims) - 1 - position))
    return loudness


def noise(rng, dims, spread, bound, shards=(), kind=jnp.bfloat16):
    loudness = block_levels(rng, dims, shards, -0.22, 0.18) if shards else 1.0
    drawn = jax.random.normal(rng, dims, jnp.float32) * spread * loudness
    return jnp.minimum(jnp.maximum(drawn, -bound), bound).astype(kind)


def setup_inputs(seed: int = 0, part: int = 0) -> dict:
    splits = jax.random.split(jax.random.key(seed), 15)
    part_splits = jax.random.split(jax.random.fold_in(splits[14], part), 15)
    return {
        "field": draw_field(jax.random.fold_in(jax.random.fold_in(splits[14], part), 71), part),
        "stale_conv_in": noise(part_splits[1], (HEIGHT, COLS, CHANNELS), 1.0, 6.0, ((0, 8),)),
        "stale_keys": noise(part_splits[2], (TOKENS, KEY_WIDTH), 1.0, 6.0, ((0, 8),)),
        "stale_values": noise(part_splits[3], (TOKENS, KEY_WIDTH), 1.0, 6.0, ((0, 8),)),
        "norm1_gain": jnp.clip(1.0 + 0.15 * jax.random.normal(splits[4], (CHANNELS,), jnp.float32), 0.25, 1.75),
        "norm1_bias": noise(splits[5], (CHANNELS,), 0.5, 3.0, (), jnp.float32),
        "conv_weight": noise(splits[6], (3, 3, CHANNELS, CHANNELS), (9 * CHANNELS) ** -0.5, 0.078125, ((3, 8),)),
        "conv_bias": noise(splits[7], (CHANNELS,), 0.5, 3.0, (), jnp.float32),
        "time_embed": noise(part_splits[8], (2, CHANNELS), 1.0, 5.0, (), jnp.float32),
        "norm2_gain": jnp.clip(1.0 + 0.15 * jax.random.normal(splits[9], (CHANNELS,), jnp.float32), 0.25, 1.75),
        "norm2_bias": noise(splits[10], (CHANNELS,), 0.5, 3.0, (), jnp.float32),
        "w_query": draw_w_query(jax.random.fold_in(splits[14], 71), part),
        "w_keyvalue": noise(splits[12], (CHANNELS, 2 * KEY_WIDTH), CHANNELS ** -0.5, 0.25),
        "w_out": noise(splits[13], (KEY_WIDTH, CHANNELS), KEY_WIDTH ** -0.5, 0.3125),
    }


epsilon = 1e-05

def group_norm(values_in, gain, bias):
    members = CHANNELS // GROUPS
    grouped = values_in.reshape(-1, GROUPS, members)
    number = grouped.shape[0] * members
    totals = lax.optimization_barrier(jnp.sum(grouped, axis=(0, 2)))
    squares = lax.optimization_barrier(jnp.sum(grouped * grouped, axis=(0, 2)))
    average = totals / number
    variance = squares / number - average * average
    scaled = (grouped - average[None, :, None]) * lax.rsqrt(variance + epsilon)[None, :, None]
    return scaled.reshape(values_in.shape) * gain + bias

def build_blocks(current_all, previous_all, parts):
    blocks = current_all.reshape(parts, -1, current_all.shape[1], current_all.shape[2])
    prior_blocks = previous_all.reshape(blocks.shape)
    zero_row = jnp.zeros_like(blocks[:1, :1])
    above = jnp.concatenate([zero_row, prior_blocks[:-1, -1:]], axis=0)
    below = jnp.concatenate([prior_blocks[1:, :1], zero_row], axis=0)
    stacked = jnp.concatenate([above, blocks, below], axis=1)
    return jnp.pad(stacked, ((0, 0), (0, 0), (1, 1), (0, 0)))

def conv_rows(padded, kernel):
    inner = padded.shape[1] - 2
    across = padded.shape[2] - 2
    result = None
    for offset_row in range(3):
        for offset_col in range(3):
            window = padded[:, offset_row:offset_row + inner, offset_col:offset_col + across, :]
            window = window.reshape(-1, padded.shape[3])
            term = jnp.dot(window, kernel[offset_row, offset_col], preferred_element_type=jnp.float32)
            result = term if result is None else result + term
    return result

def attention(query_block, key_set, value_set):
    count_rows = query_block.shape[0]
    query_heads = query_block.astype(jnp.float32).reshape(count_rows, HEADS, HEAD_DIM)
    key_heads = key_set.astype(jnp.float32).reshape(-1, HEADS, HEAD_DIM)
    value_heads = value_set.astype(jnp.float32).reshape(-1, HEADS, HEAD_DIM)
    scores = jnp.einsum('qhd,khd->hqk', query_heads, key_heads) * HEAD_DIM ** (-0.5)
    peak = lax.optimization_barrier(jnp.max(scores, axis=-1, keepdims=True))
    expo = jnp.exp(scores - peak)
    totals = lax.optimization_barrier(jnp.sum(expo, axis=-1, keepdims=True))
    weights = expo.astype(jnp.bfloat16).astype(jnp.float32)
    summed = jnp.einsum('hqk,khd->hqd', weights, value_heads) / totals
    return summed.transpose(1, 0, 2).reshape(count_rows, KEY_WIDTH).astype(jnp.bfloat16)

def attend_all(query, keys, values, prior_keys, prior_values):
    per_patch = TOKENS // N_PATCH
    owner = jnp.arange(TOKENS, dtype=jnp.int32) // per_patch

    def one_patch(index):
        chosen = (owner == index)[:, None]
        mixed_keys = jnp.where(chosen, keys, prior_keys)
        mixed_values = jnp.where(chosen, values, prior_values)
        block = lax.dynamic_slice_in_dim(query, (index * per_patch).astype(jnp.int32), per_patch, 0)
        return attention(block, mixed_keys, mixed_values)
    result = lax.map(one_patch, jnp.arange(N_PATCH, dtype=jnp.int32))
    return result.reshape(TOKENS, KEY_WIDTH)

def reference(field, stale_conv_in, stale_keys, stale_values, norm1_gain, norm1_bias, conv_weight, conv_bias, time_embed, norm2_gain, norm2_bias, w_query, w_keyvalue, w_out):
    state = field
    prior_conv = stale_conv_in
    prior_keys = stale_keys
    prior_values = stale_values
    results = []
    for which_step in range(2):
        activated = jax.nn.silu(group_norm(state, norm1_gain, norm1_bias)).astype(jnp.bfloat16)
        padded = build_blocks(activated, prior_conv, N_PATCH)
        conv_out = conv_rows(padded, conv_weight).reshape(state.shape)
        hidden = state + (conv_out + conv_bias + time_embed[which_step])
        normed = group_norm(hidden, norm2_gain, norm2_bias).astype(jnp.bfloat16).reshape(TOKENS, CHANNELS)
        query = jnp.dot(normed, w_query, preferred_element_type=jnp.float32).astype(jnp.bfloat16)
        keyvalue = jnp.dot(normed, w_keyvalue, preferred_element_type=jnp.float32).astype(jnp.bfloat16)
        keys = keyvalue[:, :KEY_WIDTH]
        values = keyvalue[:, KEY_WIDTH:]
        attended = attend_all(query, keys, values, prior_keys, prior_values)
        mixed = jnp.dot(attended, w_out, preferred_element_type=jnp.float32)
        result = hidden + mixed.reshape(hidden.shape)
        results.append(result)
        state = result
        prior_conv = activated
        prior_keys = keys
        prior_values = values
    return jnp.stack(results)
```

```python
import functools

import jax
import jax.numpy as jnp
import numpy as np
from jax import lax
from jax.experimental import pallas as pl
from jax.experimental.pallas import tpu as pltpu
from jax.sharding import PartitionSpec as P

GROUPS = 32
HEADS = 5
HEAD_DIM = 64
LANES = 128
STEPS = 2
CORES = 2

epsilon = 1e-05
MESH = pl.DeviceIdType.MESH
F32 = jnp.float32
BF16 = jnp.bfloat16


def split_rows(pair):
    high = pair.astype(BF16).astype(F32)
    rest = pair - high
    middle = rest.astype(BF16).astype(F32)
    return jnp.concatenate([high, middle, rest - middle], axis=0).astype(BF16)


def exact_dot(pair, zero_one):
    rows = pair.shape[0]
    product = jnp.dot(split_rows(pair), zero_one, preferred_element_type=F32)
    return product[:rows] + product[rows : 2 * rows] + product[2 * rows :]


def moments(values):
    return jnp.concatenate(
        [
            jnp.sum(values, axis=0, keepdims=True),
            jnp.sum(values * values, axis=0, keepdims=True),
        ],
        axis=0,
    )


def mean_and_scale(sums, number):
    average = sums[0:1] * (1.0 / number)
    variance = sums[1:2] * (1.0 / number) - average * average
    return average, lax.rsqrt(variance + epsilon)


class Gather:
    def __init__(self, parts, me, source, target, send, recv, forward_send, forward_recv):
        self.chips = parts // CORES
        self.me = me
        self.chip, self.core = me // CORES, me % CORES
        self.twin = self.chip * CORES + (1 - self.core)
        self.source, self.target = source, target
        self.sems = (send, recv, forward_send, forward_recv)

    def first(self, distance):
        send, recv, _, _ = self.sems
        peer = (
            self.twin
            if distance == 0
            else lax.rem(self.chip + distance, self.chips) * CORES + self.core
        )
        return pltpu.make_async_remote_copy(
            src_ref=self.source,
            dst_ref=self.target.at[self.me],
            send_sem=send.at[distance],
            recv_sem=recv.at[distance],
            device_id={"patch": peer},
            device_id_type=MESH,
        )

    def second(self, distance):
        _, _, send, recv = self.sems
        origin = lax.rem(self.chip - distance + self.chips, self.chips) * CORES + self.core
        return pltpu.make_async_remote_copy(
            src_ref=self.target.at[origin],
            dst_ref=self.target.at[origin],
            send_sem=send.at[distance],
            recv_sem=recv.at[distance],
            device_id={"patch": self.twin},
            device_id_type=MESH,
        )

    def start(self):
        for distance in list(range(1, self.chips)) + [0]:
            self.first(distance).start()

    def forward(self):
        for distance in range(1, self.chips):
            self.first(distance).wait_recv()
            self.second(distance).start()

    def arrive(self):
        self.first(0).wait_recv()
        for distance in range(1, self.chips):
            self.second(distance).wait_recv()

    def drain(self):
        for distance in range(self.chips):
            self.first(distance).wait_send()
        for distance in range(1, self.chips):
            self.second(distance).wait_send()


class Exchange:
    def __init__(self, parts, me, source, target, send, recv, shared=False):
        self.parts, self.me = parts, me
        self.source, self.target = source, target
        self.send, self.recv, self.shared = send, recv, shared

    def copy(self, distance):
        peer = lax.rem(self.me + distance, self.parts)
        return pltpu.make_async_remote_copy(
            src_ref=self.source if self.shared else self.source.at[peer],
            dst_ref=self.target.at[self.me],
            send_sem=self.send.at[distance],
            recv_sem=self.recv.at[distance],
            device_id={"patch": peer},
            device_id_type=MESH,
        )

    def start(self):
        for distance in sorted(range(1, self.parts), key=lambda k: -min(k, self.parts - k)):
            self.copy(distance).start()

    def arrive(self):
        for distance in range(1, self.parts):
            self.copy(distance).wait_recv()

    def drain(self):
        for distance in range(1, self.parts):
            self.copy(distance).wait_send()


def kernel(
    parts,
    field,
    stale_conv,
    stale_keys,
    stale_values,
    gain1,
    bias1,
    conv_weight,
    conv_bias,
    time_embed,
    gain2,
    bias2,
    w_query,
    w_keyvalue,
    w_out,
    to_group,
    from_group,
    same_group,
    out,
    wconv,
    wcat,
    wq,
    wkv,
    wo,
    act,
    kv_src,
    kv,
    stat_src,
    stat,
    st_src,
    st,
    nrm_src,
    nrm,
    hid_src,
    hid,
    load_sem,
    act_sem,
    kv_sem,
    x_send,
    x_recv,
):
    me = lax.axis_index("patch")
    rows, cols, channels = field.shape
    tokens = rows * cols
    share = channels // parts
    width = w_query.shape[1]
    positions = parts * tokens
    number = positions * (channels // GROUPS)

    loads = [
        pltpu.make_async_copy(source, target, load_sem.at[index])
        for index, (source, target) in enumerate(
            [(conv_weight, wconv), (w_query, wq), (w_keyvalue, wkv), (w_out, wo)]
        )
    ]
    for load in loads:
        load.start()

    barrier = pltpu.get_barrier_semaphore()
    for distance in range(1, parts):
        pl.semaphore_signal(
            barrier,
            inc=1,
            device_id={"patch": lax.rem(me + distance, parts)},
            device_id_type=MESH,
        )

    acts = [
        Gather(parts, me, act.at[i, me], act.at[i], *[act_sem.at[i, k] for k in range(4)])
        for i in range(STEPS + 1)
    ]
    kvs = [
        Gather(parts, me, source, kv.at[i], *[kv_sem.at[i, k] for k in range(4)])
        for i, source in enumerate([kv_src] + [kv.at[i, me] for i in range(STEPS - 1)])
    ]

    def exchange(kind, step, source, target, shared=False):
        return Exchange(
            parts, me, source, target, x_send.at[kind, step], x_recv.at[kind, step], shared
        )

    stats = [exchange(0, s, stat_src.at[s], stat.at[s], True) for s in range(STEPS)]
    states = [exchange(1, s, st_src.at[s], st.at[s]) for s in range(STEPS)]
    norms = [exchange(2, s, nrm_src.at[s], nrm.at[s]) for s in range(STEPS)]
    hiddens = [exchange(3, s, hid_src.at[s], hid.at[s]) for s in range(STEPS)]

    def block(values, index):
        return values[:, index * share : (index + 1) * share]

    def own_share(values):
        picked = jnp.zeros((values.shape[0], share), F32)
        for index in range(parts):
            picked = jnp.where(me == index, block(values, index), picked)
        return picked

    def send_stats(step, state):
        sums = exact_dot(moments(state), to_group[...])
        stat_src[step] = sums
        stat[step, me] = sums

    state = field[...].reshape(tokens, channels)
    send_stats(0, state)
    act[0, me] = stale_conv[...].reshape(tokens, channels)
    kv_src[...] = jnp.concatenate(
        [stale_keys[...].astype(F32), stale_values[...].astype(F32)], axis=1
    ).astype(BF16)

    pl.semaphore_wait(barrier, parts - 1)
    stats[0].start()
    acts[0].start()

    shifts = own_share(conv_bias[...] + time_embed[...])
    gain = own_share(gain2[...])
    bias = own_share(bias2[...])
    loads[0].wait()
    for tap in range(3):
        wcat[tap] = jnp.concatenate(
            [wconv[tap, k].astype(F32) for k in range(3)], axis=1
        ).astype(BF16)
    for load in loads[1:]:
        load.wait()

    column = lax.broadcasted_iota(jnp.int32, (positions, share), 0) % cols
    head_row = lax.broadcasted_iota(jnp.int32, (HEADS * tokens, width), 0) // tokens
    head_col = lax.broadcasted_iota(jnp.int32, (HEADS * tokens, width), 1) // HEAD_DIM
    on_head = head_row == head_col

    for step in range(STEPS):
        stats[step].arrive()
        average, scale = mean_and_scale(jnp.sum(stat[step], axis=0), number)
        spread = exact_dot(jnp.concatenate([average, scale], axis=0), from_group[...])
        centred = (state - spread[0:1]) * spread[1:2] * gain1[...] + bias1[...]
        act[step + 1, me] = (centred * jax.nn.sigmoid(centred)).astype(BF16)
        acts[step + 1].start()
        for index in range(parts):
            st_src[step, index] = block(state, index)
        st[step, me] = st_src[step, me]
        states[step].start()
        if step == 0:
            acts[0].forward()
            kvs[0].start()
        acts[step + 1].forward()
        if step == 0:
            acts[0].arrive()
        acts[step + 1].arrive()

        def piece(which, row):
            return act[which, row // rows, (row % rows) * cols : (row % rows + 1) * cols, :]

        whole = parts * rows
        nothing = jnp.zeros((cols, channels), BF16)
        conv = None
        for tap in range(3):
            pieces = []
            for row in range(whole):
                near = row + tap - 1
                if near < 0 or near >= whole:
                    pieces.append(nothing)
                else:
                    same = near // rows == row // rows
                    pieces.append(piece(step + 1 if same else step, near))
            term = jnp.dot(
                jnp.concatenate(pieces, axis=0), wcat[tap], preferred_element_type=F32
            )
            conv = term if conv is None else conv + term
        before = pltpu.roll(block(conv, 0), 1, 0)
        after = pltpu.roll(block(conv, 2), positions - 1, 0)
        conv = (
            block(conv, 1)
            + jnp.where(column == 0, 0.0, before)
            + jnp.where(column == cols - 1, 0.0, after)
        )
        states[step].arrive()
        hidden = st[step].reshape(positions, share) + (conv + shifts[step : step + 1])
        average, scale = mean_and_scale(exact_dot(moments(hidden), same_group[...]), number)
        normed = ((hidden - average) * scale * gain + bias).astype(BF16)
        nrm_src[step] = normed.reshape(parts, tokens, share)
        norms[step].start()
        hid_src[step] = hidden.reshape(parts, tokens, share)
        hiddens[step].start()
        nrm[step, me] = nrm_src[step, me]
        hid[step, me] = hid_src[step, me]
        if step == 0:
            kvs[0].forward()
        norms[step].arrive()
        mine = jnp.concatenate(
            [nrm[step, index].astype(F32) for index in range(parts)], axis=1
        ).astype(BF16)
        fresh = jnp.dot(mine, wkv[...], preferred_element_type=F32).astype(BF16)
        kv[step, me] = fresh
        if step + 1 < STEPS:
            kvs[step + 1].start()
        query = jnp.dot(mine, wq[...], preferred_element_type=F32).astype(BF16)
        query = jnp.concatenate([query] * HEADS, axis=0)
        query = jnp.where(on_head, query.astype(F32), 0.0).astype(BF16)
        if step > 0:
            kvs[step].forward()
        kvs[step].arrive()
        both = kv[step].reshape(positions, 2 * width)
        scores = lax.dot_general(
            query, both[:, :width], (((1,), (1,)), ((), ())), preferred_element_type=F32
        ) * HEAD_DIM ** (-0.5)
        expo = jnp.exp(scores - jnp.max(scores, axis=-1, keepdims=True))
        totals = jnp.sum(expo, axis=-1, keepdims=True)
        summed = jnp.dot(expo.astype(BF16), both, preferred_element_type=F32)[:, width:]
        summed = jnp.where(on_head, summed / totals, 0.0)
        attended = jnp.sum(summed.reshape(HEADS, tokens, width), axis=0).astype(BF16)
        mixed = jnp.dot(attended, wo[...], preferred_element_type=F32)
        hiddens[step].arrive()
        state = jnp.concatenate([hid[step, index] for index in range(parts)], axis=1) + mixed
        if step + 1 < STEPS:
            send_stats(step + 1, state)
            stats[step + 1].start()
        out[step] = state.reshape(rows, cols, channels)

    for started in acts + kvs + stats + states + norms + hiddens:
        started.drain()


def per_device(
    field,
    stale_conv_in,
    stale_keys,
    stale_values,
    norm1_gain,
    norm1_bias,
    conv_weight,
    conv_bias,
    time_embed,
    norm2_gain,
    norm2_bias,
    w_query,
    w_keyvalue,
    w_out,
):
    parts = lax.axis_size("patch")
    rows, cols, channels = field.shape
    tokens = rows * cols
    share = channels // parts
    width = w_query.shape[1]
    members = channels // GROUPS
    chips = parts // CORES
    group_of = np.arange(channels) // members
    to_group = (group_of[:, None] == np.arange(LANES)[None, :]).astype(np.float32)
    same_group = (group_of[:share, None] == group_of[None, :share]).astype(np.float32)
    vmem = pl.BlockSpec(memory_space=pltpu.VMEM)
    away = pl.BlockSpec(memory_space=pl.ANY)
    dma = pltpu.SemaphoreType.DMA
    return pl.pallas_call(
        functools.partial(kernel, parts),
        out_shape=jax.ShapeDtypeStruct((STEPS, rows, cols, channels), F32),
        in_specs=[vmem] * 6 + [away] + [vmem] * 4 + [away] * 3 + [vmem] * 3,
        out_specs=vmem,
        scratch_shapes=[
            pltpu.VMEM(conv_weight.shape, BF16),
            pltpu.VMEM((3, channels, 3 * share), BF16),
            pltpu.VMEM(w_query.shape, BF16),
            pltpu.VMEM(w_keyvalue.shape, BF16),
            pltpu.VMEM(w_out.shape, BF16),
            pltpu.VMEM((STEPS + 1, parts, tokens, channels), BF16),
            pltpu.VMEM((tokens, 2 * width), BF16),
            pltpu.VMEM((STEPS, parts, tokens, 2 * width), BF16),
            pltpu.VMEM((STEPS, 2, LANES), F32),
            pltpu.VMEM((STEPS, parts, 2, LANES), F32),
            pltpu.VMEM((STEPS, parts, tokens, share), F32),
            pltpu.VMEM((STEPS, parts, tokens, share), F32),
            pltpu.VMEM((STEPS, parts, tokens, share), BF16),
            pltpu.VMEM((STEPS, parts, tokens, share), BF16),
            pltpu.VMEM((STEPS, parts, tokens, share), F32),
            pltpu.VMEM((STEPS, parts, tokens, share), F32),
            dma((4,)),
            dma((STEPS + 1, 4, chips)),
            dma((STEPS, 4, chips)),
            dma((4, STEPS, parts)),
            dma((4, STEPS, parts)),
        ],
        compiler_params=pltpu.CompilerParams(
            collective_id=0, has_side_effects=True, vmem_limit_bytes=56 * 1024 * 1024
        ),
        cost_estimate=pl.CostEstimate(
            flops=2 * STEPS * parts * tokens * 9 * channels * share,
            bytes_accessed=2 * (9 * channels * share + 2 * channels * channels),
            transcendentals=0,
        ),
    )(
        field,
        stale_conv_in,
        stale_keys,
        stale_values,
        norm1_gain.reshape(1, -1),
        norm1_bias.reshape(1, -1),
        conv_weight,
        conv_bias.reshape(1, -1),
        time_embed,
        norm2_gain.reshape(1, -1),
        norm2_bias.reshape(1, -1),
        w_query,
        w_keyvalue,
        w_out,
        jnp.asarray(to_group, BF16),
        jnp.asarray(to_group.T, BF16),
        jnp.asarray(same_group, BF16),
    )


def solution(mesh):
    spread = ("req", "patch")
    return jax.shard_map(
        per_device,
        mesh=mesh,
        in_specs=(
            P(spread, None, None),
            P(spread, None, None),
            P(spread, None),
            P(spread, None),
            P(),
            P(),
            P(None, None, None, "patch"),
            P(),
            P("req", None),
            P(),
            P(),
            P(),
            P(),
            P(),
        ),
        out_specs=P(None, spread, None, None),
        check_vma=False,
    )
```

```python
import functools

import jax
import jax.numpy as jnp
import numpy as np
from jax import lax
from jax.experimental import pallas as pl
from jax.experimental.pallas import tpu as pltpu
from jax.sharding import PartitionSpec as P

GROUPS = 32
HEADS = 5
HEAD_DIM = 64
LANES = 128
STEPS = 2
CORES = 2

epsilon = 1e-05
MESH = pl.DeviceIdType.MESH
F32 = jnp.float32
BF16 = jnp.bfloat16


def split_rows(pair):
    high = pair.astype(BF16).astype(F32)
    rest = pair - high
    middle = rest.astype(BF16).astype(F32)
    return jnp.concatenate([high, middle, rest - middle], axis=0).astype(BF16)


def exact_dot(pair, zero_one):
    rows = pair.shape[0]
    product = jnp.dot(split_rows(pair), zero_one, preferred_element_type=F32)
    return product[:rows] + product[rows : 2 * rows] + product[2 * rows :]


def dot_transposed(left, right):
    return lax.dot_general(
        left, right, (((1,), (1,)), ((), ())), preferred_element_type=F32
    )


def moments(values):
    return jnp.concatenate(
        [
            jnp.sum(values, axis=0, keepdims=True),
            jnp.sum(values * values, axis=0, keepdims=True),
        ],
        axis=0,
    )


def mean_and_scale(sums, number):
    average = sums[0:1] * (1.0 / number)
    variance = sums[1:2] * (1.0 / number) - average * average
    return average, lax.rsqrt(variance + epsilon)


class Gather:
    def __init__(self, parts, me, source, target, send, recv, forward_send, forward_recv):
        self.chips = parts // CORES
        self.me = me
        self.chip, self.core = me // CORES, me % CORES
        self.twin = self.chip * CORES + (1 - self.core)
        self.source, self.target = source, target
        self.sems = (send, recv, forward_send, forward_recv)

    def first(self, distance):
        send, recv, _, _ = self.sems
        peer = (
            self.twin
            if distance == 0
            else lax.rem(self.chip + distance, self.chips) * CORES + self.core
        )
        return pltpu.make_async_remote_copy(
            src_ref=self.source,
            dst_ref=self.target.at[self.me],
            send_sem=send.at[distance],
            recv_sem=recv.at[distance],
            device_id={"patch": peer},
            device_id_type=MESH,
        )

    def second(self, distance):
        _, _, send, recv = self.sems
        origin = lax.rem(self.chip - distance + self.chips, self.chips) * CORES + self.core
        return pltpu.make_async_remote_copy(
            src_ref=self.target.at[origin],
            dst_ref=self.target.at[origin],
            send_sem=send.at[distance],
            recv_sem=recv.at[distance],
            device_id={"patch": self.twin},
            device_id_type=MESH,
        )

    def start(self):
        for distance in list(range(1, self.chips)) + [0]:
            self.first(distance).start()

    def forward(self):
        for distance in range(1, self.chips):
            self.first(distance).wait_recv()
            self.second(distance).start()

    def arrive(self):
        self.first(0).wait_recv()
        for distance in range(1, self.chips):
            self.second(distance).wait_recv()

    def drain(self):
        for distance in range(self.chips):
            self.first(distance).wait_send()
        for distance in range(1, self.chips):
            self.second(distance).wait_send()


class Exchange:
    def __init__(self, parts, me, source, target, send, recv, shared=False):
        self.parts, self.me = parts, me
        self.source, self.target = source, target
        self.send, self.recv, self.shared = send, recv, shared

    def copy(self, distance):
        peer = lax.rem(self.me + distance, self.parts)
        return pltpu.make_async_remote_copy(
            src_ref=self.source if self.shared else self.source.at[peer],
            dst_ref=self.target.at[self.me],
            send_sem=self.send.at[distance],
            recv_sem=self.recv.at[distance],
            device_id={"patch": peer},
            device_id_type=MESH,
        )

    def start(self):
        for distance in sorted(range(1, self.parts), key=lambda k: -min(k, self.parts - k)):
            self.copy(distance).start()

    def arrive(self):
        for distance in range(1, self.parts):
            self.copy(distance).wait_recv()

    def drain(self):
        for distance in range(1, self.parts):
            self.copy(distance).wait_send()


def kernel(
    parts,
    field,
    stale_conv,
    stale_keys,
    stale_values,
    gain1,
    bias1,
    conv_weight,
    conv_bias,
    time_embed,
    gain2,
    bias2,
    w_query,
    w_keyvalue,
    w_out,
    to_group,
    from_group,
    same_group,
    out,
    wconv,
    wq,
    wkv,
    wo,
    act,
    kv_src,
    kv,
    stat_src,
    stat,
    st_src,
    st,
    nrm_src,
    nrm,
    hid_src,
    hid,
    load_sem,
    act_sem,
    kv_sem,
    x_send,
    x_recv,
):
    me = lax.axis_index("patch")
    rows, cols, channels = field.shape
    tokens = rows * cols
    share = channels // parts
    width = w_query.shape[0]
    positions = parts * tokens
    number = positions * (channels // GROUPS)

    loads = [
        pltpu.make_async_copy(source, target, load_sem.at[index])
        for index, (source, target) in enumerate(
            [(conv_weight, wconv), (w_query, wq), (w_keyvalue, wkv), (w_out, wo)]
        )
    ]
    for load in loads:
        load.start()

    barrier = pltpu.get_barrier_semaphore()
    for distance in range(1, parts):
        pl.semaphore_signal(
            barrier,
            inc=1,
            device_id={"patch": lax.rem(me + distance, parts)},
            device_id_type=MESH,
        )

    acts = [
        Gather(parts, me, act.at[i, me], act.at[i], *[act_sem.at[i, k] for k in range(4)])
        for i in range(STEPS + 1)
    ]
    kvs = [
        Gather(parts, me, source, kv.at[i], *[kv_sem.at[i, k] for k in range(4)])
        for i, source in enumerate([kv_src] + [kv.at[i, me] for i in range(STEPS - 1)])
    ]

    def exchange(kind, step, source, target, shared=False):
        return Exchange(
            parts, me, source, target, x_send.at[kind, step], x_recv.at[kind, step], shared
        )

    stats = [exchange(0, s, stat_src.at[s], stat.at[s], True) for s in range(STEPS)]
    states = [exchange(1, s, st_src.at[s], st.at[s]) for s in range(STEPS)]
    norms = [exchange(2, s, nrm_src.at[s], nrm.at[s]) for s in range(STEPS)]
    hiddens = [exchange(3, s, hid_src.at[s], hid.at[s]) for s in range(STEPS)]

    def block(values, index):
        return values[:, index * share : (index + 1) * share]

    def own_share(values):
        picked = jnp.zeros((values.shape[0], share), F32)
        for index in range(parts):
            picked = jnp.where(me == index, block(values, index), picked)
        return picked

    def send_stats(step, state):
        sums = exact_dot(moments(state), to_group[...])
        stat_src[step] = sums
        stat[step, me] = sums

    state = field[...].reshape(tokens, channels)
    send_stats(0, state)
    act[0, me] = stale_conv[...].reshape(tokens, channels)
    kv_src[...] = jnp.concatenate(
        [stale_keys[...].astype(F32), stale_values[...].astype(F32)], axis=1
    ).astype(BF16)

    pl.semaphore_wait(barrier, parts - 1)
    stats[0].start()
    acts[0].start()

    shifts = own_share(conv_bias[...][None, :] + time_embed[...])
    gain = own_share(gain2[...][None, :])
    bias = own_share(bias2[...][None, :])
    loads[0].wait()
    for load in loads[1:]:
        load.wait()

    column = lax.broadcasted_iota(jnp.int32, (positions, share), 0) % cols
    head_row = lax.broadcasted_iota(jnp.int32, (HEADS * tokens, width), 0) // tokens
    head_col = lax.broadcasted_iota(jnp.int32, (HEADS * tokens, width), 1) // HEAD_DIM
    on_head = head_row == head_col

    for step in range(STEPS):
        stats[step].arrive()
        average, scale = mean_and_scale(jnp.sum(stat[step], axis=0), number)
        spread = exact_dot(jnp.concatenate([average, scale], axis=0), from_group[...])
        centred = (state - spread[0:1]) * spread[1:2] * gain1[...][None, :] + bias1[...][None, :]
        act[step + 1, me] = (centred * jax.nn.sigmoid(centred)).astype(BF16)
        acts[step + 1].start()
        for index in range(parts):
            st_src[step, index] = block(state, index)
        st[step, me] = st_src[step, me]
        states[step].start()
        if step == 0:
            acts[0].forward()
            kvs[0].start()
        acts[step + 1].forward()
        if step == 0:
            acts[0].arrive()
        acts[step + 1].arrive()

        def piece(which, row):
            return act[which, row // rows, (row % rows) * cols : (row % rows + 1) * cols, :]

        whole = parts * rows
        nothing = jnp.zeros((cols, channels), BF16)
        conv = None
        for tap in range(3):
            pieces = []
            for row in range(whole):
                near = row + tap - 1
                if near < 0 or near >= whole:
                    pieces.append(nothing)
                else:
                    same = near // rows == row // rows
                    pieces.append(piece(step + 1 if same else step, near))
            term = dot_transposed(
                jnp.concatenate(pieces, axis=0), wconv[tap].reshape(3 * share, channels)
            )
            conv = term if conv is None else conv + term
        before = pltpu.roll(block(conv, 0), 1, 0)
        after = pltpu.roll(block(conv, 2), positions - 1, 0)
        conv = (
            block(conv, 1)
            + jnp.where(column == 0, 0.0, before)
            + jnp.where(column == cols - 1, 0.0, after)
        )
        states[step].arrive()
        hidden = st[step].reshape(positions, share) + (conv + shifts[step : step + 1])
        average, scale = mean_and_scale(exact_dot(moments(hidden), same_group[...]), number)
        normed = ((hidden - average) * scale * gain + bias).astype(BF16)
        nrm_src[step] = normed.reshape(parts, tokens, share)
        norms[step].start()
        hid_src[step] = hidden.reshape(parts, tokens, share)
        hiddens[step].start()
        nrm[step, me] = nrm_src[step, me]
        hid[step, me] = hid_src[step, me]
        if step == 0:
            kvs[0].forward()
        norms[step].arrive()
        mine = jnp.concatenate(
            [nrm[step, index].astype(F32) for index in range(parts)], axis=1
        ).astype(BF16)
        fresh = jnp.dot(mine, wkv[...], preferred_element_type=F32).astype(BF16)
        kv[step, me] = fresh
        if step + 1 < STEPS:
            kvs[step + 1].start()
        query = dot_transposed(mine, wq[...]).astype(BF16)
        query = jnp.concatenate([query] * HEADS, axis=0)
        query = jnp.where(on_head, query.astype(F32), 0.0).astype(BF16)
        if step > 0:
            kvs[step].forward()
        kvs[step].arrive()
        both = kv[step].reshape(positions, 2 * width)
        scores = dot_transposed(query, both[:, :width]) * HEAD_DIM ** (-0.5)
        expo = jnp.exp(scores - jnp.max(scores, axis=-1, keepdims=True))
        totals = jnp.sum(expo, axis=-1, keepdims=True)
        summed = jnp.dot(expo.astype(BF16), both, preferred_element_type=F32)[:, width:]
        summed = jnp.where(on_head, summed / totals, 0.0)
        attended = jnp.sum(summed.reshape(HEADS, tokens, width), axis=0).astype(BF16)
        mixed = jnp.dot(attended, wo[...], preferred_element_type=F32)
        hiddens[step].arrive()
        state = jnp.concatenate([hid[step, index] for index in range(parts)], axis=1) + mixed
        if step + 1 < STEPS:
            send_stats(step + 1, state)
            stats[step + 1].start()
        out[step] = state.reshape(rows, cols, channels)

    for started in acts + kvs + stats + states + norms + hiddens:
        started.drain()


def per_device(
    field,
    stale_conv_in,
    stale_keys,
    stale_values,
    norm1_gain,
    norm1_bias,
    conv_weight,
    conv_bias,
    time_embed,
    norm2_gain,
    norm2_bias,
    w_query,
    w_keyvalue,
    w_out,
):
    parts = lax.axis_size("patch")
    rows, cols, channels = field.shape
    tokens = rows * cols
    share = channels // parts
    width = w_query.shape[1]
    members = channels // GROUPS
    chips = parts // CORES
    group_of = np.arange(channels) // members
    to_group = (group_of[:, None] == np.arange(LANES)[None, :]).astype(np.float32)
    same_group = (group_of[:share, None] == group_of[None, :share]).astype(np.float32)
    vmem = pl.BlockSpec(memory_space=pltpu.VMEM)
    away = pl.BlockSpec(memory_space=pl.ANY)
    dma = pltpu.SemaphoreType.DMA
    return pl.pallas_call(
        functools.partial(kernel, parts),
        out_shape=jax.ShapeDtypeStruct((STEPS, rows, cols, channels), F32),
        in_specs=[vmem] * 6 + [away] + [vmem] * 4 + [away] * 3 + [vmem] * 3,
        out_specs=vmem,
        scratch_shapes=[
            pltpu.VMEM((3, 3, share, channels), BF16),
            pltpu.VMEM((width, channels), BF16),
            pltpu.VMEM(w_keyvalue.shape, BF16),
            pltpu.VMEM(w_out.shape, BF16),
            pltpu.VMEM((STEPS + 1, parts, tokens, channels), BF16),
            pltpu.VMEM((tokens, 2 * width), BF16),
            pltpu.VMEM((STEPS, parts, tokens, 2 * width), BF16),
            pltpu.VMEM((STEPS, 2, LANES), F32),
            pltpu.VMEM((STEPS, parts, 2, LANES), F32),
            pltpu.VMEM((STEPS, parts, tokens, share), F32),
            pltpu.VMEM((STEPS, parts, tokens, share), F32),
            pltpu.VMEM((STEPS, parts, tokens, share), BF16),
            pltpu.VMEM((STEPS, parts, tokens, share), BF16),
            pltpu.VMEM((STEPS, parts, tokens, share), F32),
            pltpu.VMEM((STEPS, parts, tokens, share), F32),
            dma((4,)),
            dma((STEPS + 1, 4, chips)),
            dma((STEPS, 4, chips)),
            dma((4, STEPS, parts)),
            dma((4, STEPS, parts)),
        ],
        compiler_params=pltpu.CompilerParams(
            collective_id=0, has_side_effects=True, vmem_limit_bytes=56 * 1024 * 1024
        ),
        cost_estimate=pl.CostEstimate(
            flops=2 * STEPS * parts * tokens * 9 * channels * share,
            bytes_accessed=2 * (9 * channels * share + 2 * channels * channels),
            transcendentals=0,
        ),
    )(
        field,
        stale_conv_in,
        stale_keys,
        stale_values,
        norm1_gain,
        norm1_bias,
        conv_weight.transpose(0, 1, 3, 2),
        conv_bias,
        time_embed,
        norm2_gain,
        norm2_bias,
        w_query.T,
        w_keyvalue,
        w_out,
        jnp.asarray(to_group, BF16),
        jnp.asarray(to_group.T, BF16),
        jnp.asarray(same_group, BF16),
    )


def solution(mesh):
    spread = ("req", "patch")
    return jax.shard_map(
        per_device,
        mesh=mesh,
        in_specs=(
            P(spread, None, None),
            P(spread, None, None),
            P(spread, None),
            P(spread, None),
            P(),
            P(),
            P(None, None, None, "patch"),
            P(),
            P("req", None),
            P(),
            P(),
            P(),
            P(),
            P(),
        ),
        out_specs=P(None, spread, None, None),
        check_vma=False,
    )
```

```python
import functools

import jax
import jax.numpy as jnp
import numpy as np
from jax import lax
from jax.experimental import pallas as pl
from jax.experimental.pallas import tpu as pltpu
from jax.sharding import PartitionSpec as P

GROUPS = 32
HEADS = 5
HEAD_DIM = 64
LANES = 128
STEPS = 2
CORES = 2

epsilon = 1e-05
MESH = pl.DeviceIdType.MESH
F32 = jnp.float32
BF16 = jnp.bfloat16


def split_rows(pair):
    high = pair.astype(BF16).astype(F32)
    rest = pair - high
    middle = rest.astype(BF16).astype(F32)
    return jnp.concatenate([high, middle, rest - middle], axis=0).astype(BF16)


def exact_dot(pair, zero_one):
    rows = pair.shape[0]
    product = jnp.dot(split_rows(pair), zero_one, preferred_element_type=F32)
    return product[:rows] + product[rows : 2 * rows] + product[2 * rows :]


def dot_transposed(left, right):
    return lax.dot_general(
        left, right, (((1,), (1,)), ((), ())), preferred_element_type=F32
    )


def moments(values):
    return jnp.concatenate(
        [
            jnp.sum(values, axis=0, keepdims=True),
            jnp.sum(values * values, axis=0, keepdims=True),
        ],
        axis=0,
    )


def mean_and_scale(sums, number):
    average = sums[0:1] * (1.0 / number)
    variance = sums[1:2] * (1.0 / number) - average * average
    return average, lax.rsqrt(variance + epsilon)


class Gather:
    def __init__(self, parts, me, source, target, send, recv, forward_send, forward_recv):
        self.chips = parts // CORES
        self.me = me
        self.chip, self.core = me // CORES, me % CORES
        self.twin = self.chip * CORES + (1 - self.core)
        self.source, self.target = source, target
        self.sems = (send, recv, forward_send, forward_recv)

    def first(self, distance):
        send, recv, _, _ = self.sems
        peer = (
            self.twin
            if distance == 0
            else lax.rem(self.chip + distance, self.chips) * CORES + self.core
        )
        return pltpu.make_async_remote_copy(
            src_ref=self.source,
            dst_ref=self.target.at[self.me],
            send_sem=send.at[distance],
            recv_sem=recv.at[distance],
            device_id={"patch": peer},
            device_id_type=MESH,
        )

    def second(self, distance):
        _, _, send, recv = self.sems
        origin = lax.rem(self.chip - distance + self.chips, self.chips) * CORES + self.core
        return pltpu.make_async_remote_copy(
            src_ref=self.target.at[origin],
            dst_ref=self.target.at[origin],
            send_sem=send.at[distance],
            recv_sem=recv.at[distance],
            device_id={"patch": self.twin},
            device_id_type=MESH,
        )

    def start(self):
        for distance in list(range(1, self.chips)) + [0]:
            self.first(distance).start()

    def forward(self):
        for distance in range(1, self.chips):
            self.first(distance).wait_recv()
            self.second(distance).start()

    def walk(self, use):
        use(self.me)
        self.first(0).wait_recv()
        use(self.twin)
        for distance in range(1, self.chips):
            self.first(distance).wait_recv()
            self.second(distance).start()
            use(lax.rem(self.chip - distance + self.chips, self.chips) * CORES + self.core)
        for distance in range(1, self.chips):
            self.second(distance).wait_recv()
            use(lax.rem(self.chip - distance + self.chips, self.chips) * CORES + 1 - self.core)

    def arrive(self):
        self.first(0).wait_recv()
        for distance in range(1, self.chips):
            self.second(distance).wait_recv()

    def drain(self):
        for distance in range(self.chips):
            self.first(distance).wait_send()
        for distance in range(1, self.chips):
            self.second(distance).wait_send()


class Exchange:
    def __init__(self, parts, me, source, target, send, recv, shared=False):
        self.parts, self.me = parts, me
        self.source, self.target = source, target
        self.send, self.recv, self.shared = send, recv, shared

    def copy(self, distance):
        peer = lax.rem(self.me + distance, self.parts)
        return pltpu.make_async_remote_copy(
            src_ref=self.source if self.shared else self.source.at[peer],
            dst_ref=self.target.at[self.me],
            send_sem=self.send.at[distance],
            recv_sem=self.recv.at[distance],
            device_id={"patch": peer},
            device_id_type=MESH,
        )

    def start(self):
        for distance in sorted(range(1, self.parts), key=lambda k: -min(k, self.parts - k)):
            self.copy(distance).start()

    def arrive(self):
        for distance in range(1, self.parts):
            self.copy(distance).wait_recv()

    def drain(self):
        for distance in range(1, self.parts):
            self.copy(distance).wait_send()


def kernel(
    parts,
    field,
    stale_conv,
    stale_keys,
    stale_values,
    gain1,
    bias1,
    conv_weight,
    conv_bias,
    time_embed,
    gain2,
    bias2,
    w_query,
    w_keyvalue,
    w_out,
    to_group,
    from_group,
    same_group,
    out,
    wconv,
    wq,
    wkv,
    wo,
    act,
    kv_src,
    kv,
    stat,
    cen,
    nrm_src,
    nrm,
    hid_src,
    hid,
    load_sem,
    act_sem,
    stat_sem,
    cen_sem,
    kv_sem,
    x_send,
    x_recv,
):
    me = lax.axis_index("patch")
    rows, cols, channels = field.shape
    tokens = rows * cols
    share = channels // parts
    width = w_query.shape[0]
    positions = parts * tokens
    number = positions * (channels // GROUPS)

    loads = [
        pltpu.make_async_copy(source, target, load_sem.at[index])
        for index, (source, target) in enumerate(
            [(conv_weight, wconv), (w_query, wq), (w_keyvalue, wkv), (w_out, wo)]
        )
    ]
    for load in loads:
        load.start()

    barrier = pltpu.get_barrier_semaphore()
    for distance in range(1, parts):
        pl.semaphore_signal(
            barrier,
            inc=1,
            device_id={"patch": lax.rem(me + distance, parts)},
            device_id_type=MESH,
        )

    def gather(block_of, sems, i):
        return Gather(parts, me, block_of.at[i, me], block_of.at[i], *[sems.at[i, k] for k in range(4)])

    acts = [
        Gather(parts, me, act.at[0, me], act.at[0], *[act_sem.at[k] for k in range(4)])
    ]
    stats = [gather(stat, stat_sem, step) for step in range(STEPS)]
    cens = [gather(cen, cen_sem, step) for step in range(STEPS)]
    kvs = [
        Gather(parts, me, source, kv.at[i], *[kv_sem.at[i, k] for k in range(4)])
        for i, source in enumerate([kv_src] + [kv.at[i, me] for i in range(STEPS - 1)])
    ]

    def exchange(kind, step, source, target, shared=False):
        return Exchange(
            parts, me, source, target, x_send.at[kind, step], x_recv.at[kind, step], shared
        )

    norms = [exchange(0, s, nrm_src.at[s], nrm.at[s]) for s in range(STEPS)]
    hiddens = [exchange(1, s, hid_src.at[s], hid.at[s]) for s in range(STEPS)]

    def block(values, index):
        return values[:, index * share : (index + 1) * share]

    def own_share(values):
        picked = jnp.zeros((values.shape[0], share), F32)
        for index in range(parts):
            picked = jnp.where(me == index, block(values, index), picked)
        return picked

    def send_state(step, state):
        sums = moments(state)
        stat[step, me] = sums
        if step > 0:
            stats[step].start()
        cen[step, me] = (state - sums[0:1] * (1.0 / tokens)).astype(BF16)
        if step > 0:
            cens[step].start()

    state = field[...].reshape(tokens, channels)
    send_state(0, state)
    act[0, me] = stale_conv[...].reshape(tokens, channels)
    kv_src[...] = jnp.concatenate(
        [stale_keys[...].astype(F32), stale_values[...].astype(F32)], axis=1
    ).astype(BF16)

    pl.semaphore_wait(barrier, parts - 1)
    for started in (stats[0], cens[0], acts[0], kvs[0]):
        started.start()

    row_shifts = conv_bias[...][None, :] + time_embed[...]
    shifts = own_share(row_shifts)
    gain = own_share(gain2[...][None, :])
    bias = own_share(bias2[...][None, :])
    loads[0].wait()
    for load in loads[1:]:
        load.wait()

    pick = jnp.where(
        lax.broadcasted_iota(jnp.int32, (channels, share), 0) - me * share
        == lax.broadcasted_iota(jnp.int32, (channels, share), 1),
        1.0,
        0.0,
    ).astype(BF16)
    column = lax.broadcasted_iota(jnp.int32, (positions, share), 0) % cols
    head_row = lax.broadcasted_iota(jnp.int32, (HEADS * tokens, width), 0) // tokens
    head_col = lax.broadcasted_iota(jnp.int32, (HEADS * tokens, width), 1) // HEAD_DIM
    on_head = head_row == head_col

    for step in range(STEPS):
        stats[step].forward()
        stats[step].arrive()
        sums = exact_dot(jnp.sum(stat[step], axis=0), to_group[...])
        average, scale = mean_and_scale(sums, number)
        spread = exact_dot(jnp.concatenate([average, scale], axis=0), from_group[...])
        slope = spread[1:2] * gain1[...][None, :]
        average = spread[0:1]

        def activate(which):
            mean = stat[step, which][0:1] * (1.0 / tokens)
            offset = (mean - average) * slope + bias1[...][None, :]
            value = cen[step, which].astype(F32) * slope + offset
            act[step + 1, which] = (value * jax.nn.sigmoid(value)).astype(BF16)

        cens[step].walk(activate)
        means = stat[step][:, 0, :] * (1.0 / tokens)
        held = jnp.dot(
            cen[step].reshape(positions, channels), pick, preferred_element_type=F32
        ).reshape(parts, tokens, share) + exact_dot(means, pick)[:, None, :]
        if step == 0:
            acts[0].forward()
            acts[0].arrive()

        def piece(which, row):
            return act[which, row // rows, (row % rows) * cols : (row % rows + 1) * cols, :]

        whole = parts * rows
        nothing = jnp.zeros((cols, channels), BF16)
        conv = None
        for tap in range(3):
            pieces = []
            for row in range(whole):
                near = row + tap - 1
                if near < 0 or near >= whole:
                    pieces.append(nothing)
                else:
                    same = near // rows == row // rows
                    pieces.append(piece(step + 1 if same else step, near))
            term = dot_transposed(
                jnp.concatenate(pieces, axis=0), wconv[tap].reshape(3 * share, channels)
            )
            conv = term if conv is None else conv + term
        before = pltpu.roll(block(conv, 0), 1, 0)
        after = pltpu.roll(block(conv, 2), positions - 1, 0)
        conv = (
            block(conv, 1)
            + jnp.where(column == 0, 0.0, before)
            + jnp.where(column == cols - 1, 0.0, after)
        )
        hidden = held.reshape(positions, share) + (conv + shifts[step : step + 1])
        average, scale = mean_and_scale(exact_dot(moments(hidden), same_group[...]), number)
        normed = ((hidden - average) * scale * gain + bias).astype(BF16)
        nrm_src[step] = normed.reshape(parts, tokens, share)
        norms[step].start()
        hid_src[step] = conv.astype(BF16).reshape(parts, tokens, share)
        hiddens[step].start()
        nrm[step, me] = nrm_src[step, me]
        hid[step, me] = hid_src[step, me]
        if step == 0:
            kvs[0].forward()
        norms[step].arrive()
        mine = jnp.concatenate(
            [nrm[step, index].astype(F32) for index in range(parts)], axis=1
        ).astype(BF16)
        fresh = jnp.dot(mine, wkv[...], preferred_element_type=F32).astype(BF16)
        kv[step, me] = fresh
        if step + 1 < STEPS:
            kvs[step + 1].start()
        query = dot_transposed(mine, wq[...]).astype(BF16)
        query = jnp.concatenate([query] * HEADS, axis=0)
        query = jnp.where(on_head, query.astype(F32), 0.0).astype(BF16)
        if step > 0:
            kvs[step].forward()
        kvs[step].arrive()
        both = kv[step].reshape(positions, 2 * width)
        scores = dot_transposed(query, both[:, :width]) * HEAD_DIM ** (-0.5)
        expo = jnp.exp(scores - jnp.max(scores, axis=-1, keepdims=True))
        totals = jnp.sum(expo, axis=-1, keepdims=True)
        summed = jnp.dot(expo.astype(BF16), both, preferred_element_type=F32)[:, width:]
        summed = jnp.where(on_head, summed / totals, 0.0)
        attended = jnp.sum(summed.reshape(HEADS, tokens, width), axis=0).astype(BF16)
        mixed = jnp.dot(attended, wo[...], preferred_element_type=F32)
        hiddens[step].arrive()
        convolved = jnp.concatenate(
            [hid[step, index].astype(F32) for index in range(parts)], axis=1
        )
        state = (state + (convolved + row_shifts[step : step + 1])) + mixed
        if step + 1 < STEPS:
            send_state(step + 1, state)
        out[step] = state.reshape(rows, cols, channels)

    for started in acts + kvs + stats + cens + norms + hiddens:
        started.drain()


def per_device(
    field,
    stale_conv_in,
    stale_keys,
    stale_values,
    norm1_gain,
    norm1_bias,
    conv_weight,
    conv_bias,
    time_embed,
    norm2_gain,
    norm2_bias,
    w_query,
    w_keyvalue,
    w_out,
):
    parts = lax.axis_size("patch")
    rows, cols, channels = field.shape
    tokens = rows * cols
    share = channels // parts
    width = w_query.shape[1]
    members = channels // GROUPS
    chips = parts // CORES
    group_of = np.arange(channels) // members
    to_group = (group_of[:, None] == np.arange(LANES)[None, :]).astype(np.float32)
    same_group = (group_of[:share, None] == group_of[None, :share]).astype(np.float32)
    vmem = pl.BlockSpec(memory_space=pltpu.VMEM)
    away = pl.BlockSpec(memory_space=pl.ANY)
    dma = pltpu.SemaphoreType.DMA
    return pl.pallas_call(
        functools.partial(kernel, parts),
        out_shape=jax.ShapeDtypeStruct((STEPS, rows, cols, channels), F32),
        in_specs=[vmem] * 6 + [away] + [vmem] * 4 + [away] * 3 + [vmem] * 3,
        out_specs=vmem,
        scratch_shapes=[
            pltpu.VMEM((3, 3, share, channels), BF16),
            pltpu.VMEM((width, channels), BF16),
            pltpu.VMEM(w_keyvalue.shape, BF16),
            pltpu.VMEM(w_out.shape, BF16),
            pltpu.VMEM((STEPS + 1, parts, tokens, channels), BF16),
            pltpu.VMEM((tokens, 2 * width), BF16),
            pltpu.VMEM((STEPS, parts, tokens, 2 * width), BF16),
            pltpu.VMEM((STEPS, parts, 2, channels), F32),
            pltpu.VMEM((STEPS, parts, tokens, channels), BF16),
            pltpu.VMEM((STEPS, parts, tokens, share), BF16),
            pltpu.VMEM((STEPS, parts, tokens, share), BF16),
            pltpu.VMEM((STEPS, parts, tokens, share), BF16),
            pltpu.VMEM((STEPS, parts, tokens, share), BF16),
            dma((4,)),
            dma((4, chips)),
            dma((STEPS, 4, chips)),
            dma((STEPS, 4, chips)),
            dma((STEPS, 4, chips)),
            dma((2, STEPS, parts)),
            dma((2, STEPS, parts)),
        ],
        compiler_params=pltpu.CompilerParams(
            collective_id=0, has_side_effects=True, vmem_limit_bytes=56 * 1024 * 1024
        ),
        cost_estimate=pl.CostEstimate(
            flops=2 * STEPS * parts * tokens * 9 * channels * share,
            bytes_accessed=2 * (9 * channels * share + 2 * channels * channels),
            transcendentals=0,
        ),
    )(
        field,
        stale_conv_in,
        stale_keys,
        stale_values,
        norm1_gain,
        norm1_bias,
        conv_weight.transpose(0, 1, 3, 2),
        conv_bias,
        time_embed,
        norm2_gain,
        norm2_bias,
        w_query.T,
        w_keyvalue,
        w_out,
        jnp.asarray(to_group, BF16),
        jnp.asarray(to_group.T, BF16),
        jnp.asarray(same_group, BF16),
    )


def solution(mesh):
    spread = ("req", "patch")
    return jax.shard_map(
        per_device,
        mesh=mesh,
        in_specs=(
            P(spread, None, None),
            P(spread, None, None),
            P(spread, None),
            P(spread, None),
            P(),
            P(),
            P(None, None, None, "patch"),
            P(),
            P("req", None),
            P(),
            P(),
            P(),
            P(),
            P(),
        ),
        out_specs=P(None, spread, None, None),
        check_vma=False,
    )
```

```python
import functools

import jax
import jax.numpy as jnp
import numpy as np
from jax import lax
from jax.experimental import pallas as pl
from jax.experimental.pallas import tpu as pltpu
from jax.sharding import PartitionSpec as P

GROUPS = 32
HEADS = 5
HEAD_DIM = 64
LANES = 128
STEPS = 2
CORES = 2

epsilon = 1e-05
MESH = pl.DeviceIdType.MESH
F32 = jnp.float32
BF16 = jnp.bfloat16


def split_rows(pair):
    high = pair.astype(BF16).astype(F32)
    rest = pair - high
    middle = rest.astype(BF16).astype(F32)
    return jnp.concatenate([high, middle, rest - middle], axis=0).astype(BF16)


def exact_dot(pair, zero_one):
    rows = pair.shape[0]
    product = jnp.dot(split_rows(pair), zero_one, preferred_element_type=F32)
    return product[:rows] + product[rows : 2 * rows] + product[2 * rows :]


def dot_transposed(left, right):
    return lax.dot_general(
        left, right, (((1,), (1,)), ((), ())), preferred_element_type=F32
    )


def moments(values):
    return jnp.concatenate(
        [
            jnp.sum(values, axis=0, keepdims=True),
            jnp.sum(values * values, axis=0, keepdims=True),
        ],
        axis=0,
    )


def mean_and_scale(sums, number):
    average = sums[0:1] * (1.0 / number)
    variance = sums[1:2] * (1.0 / number) - average * average
    return average, lax.rsqrt(variance + epsilon)


class Gather:
    def __init__(self, parts, me, source, target, send, recv, forward_send, forward_recv):
        self.chips = parts // CORES
        self.me = me
        self.chip, self.core = me // CORES, me % CORES
        self.twin = self.chip * CORES + (1 - self.core)
        self.source, self.target = source, target
        self.sems = (send, recv, forward_send, forward_recv)

    def first(self, distance):
        send, recv, _, _ = self.sems
        peer = (
            self.twin
            if distance == 0
            else lax.rem(self.chip + distance, self.chips) * CORES + self.core
        )
        return pltpu.make_async_remote_copy(
            src_ref=self.source,
            dst_ref=self.target.at[self.me],
            send_sem=send.at[distance],
            recv_sem=recv.at[distance],
            device_id={"patch": peer},
            device_id_type=MESH,
        )

    def second(self, distance):
        _, _, send, recv = self.sems
        origin = lax.rem(self.chip - distance + self.chips, self.chips) * CORES + self.core
        return pltpu.make_async_remote_copy(
            src_ref=self.target.at[origin],
            dst_ref=self.target.at[origin],
            send_sem=send.at[distance],
            recv_sem=recv.at[distance],
            device_id={"patch": self.twin},
            device_id_type=MESH,
        )

    def start(self):
        for distance in list(range(1, self.chips)) + [0]:
            self.first(distance).start()

    def forward(self):
        for distance in range(1, self.chips):
            self.first(distance).wait_recv()
            self.second(distance).start()

    def walk(self, use):
        use(self.me)
        self.first(0).wait_recv()
        use(self.twin)
        for distance in range(1, self.chips):
            self.first(distance).wait_recv()
            self.second(distance).start()
            use(lax.rem(self.chip - distance + self.chips, self.chips) * CORES + self.core)
        for distance in range(1, self.chips):
            self.second(distance).wait_recv()
            use(lax.rem(self.chip - distance + self.chips, self.chips) * CORES + 1 - self.core)

    def arrive(self):
        self.first(0).wait_recv()
        for distance in range(1, self.chips):
            self.second(distance).wait_recv()

    def drain(self):
        for distance in range(self.chips):
            self.first(distance).wait_send()
        for distance in range(1, self.chips):
            self.second(distance).wait_send()


class Exchange:
    def __init__(self, parts, me, source, target, send, recv, shared=False):
        self.parts, self.me = parts, me
        self.source, self.target = source, target
        self.send, self.recv, self.shared = send, recv, shared

    def copy(self, distance):
        peer = lax.rem(self.me + distance, self.parts)
        return pltpu.make_async_remote_copy(
            src_ref=self.source if self.shared else self.source.at[peer],
            dst_ref=self.target.at[self.me],
            send_sem=self.send.at[distance],
            recv_sem=self.recv.at[distance],
            device_id={"patch": peer},
            device_id_type=MESH,
        )

    def start(self):
        for distance in sorted(range(1, self.parts), key=lambda k: -min(k, self.parts - k)):
            self.copy(distance).start()

    def arrive(self):
        for distance in range(1, self.parts):
            self.copy(distance).wait_recv()

    def drain(self):
        for distance in range(1, self.parts):
            self.copy(distance).wait_send()


def kernel(
    parts,
    field,
    stale_conv,
    stale_keys,
    stale_values,
    gain1,
    bias1,
    conv_weight,
    conv_bias,
    time_embed,
    gain2,
    bias2,
    w_query,
    w_keyvalue,
    w_out,
    to_group,
    from_group,
    same_group,
    out,
    wconv,
    wq,
    wkv,
    wo,
    act,
    kv_src,
    kv,
    stat,
    cen,
    nrm_src,
    nrm,
    hid_src,
    hid,
    load_sem,
    act_sem,
    stat_sem,
    cen_sem,
    kv_sem,
    x_send,
    x_recv,
):
    me = lax.axis_index("patch")
    rows, cols, channels = field.shape
    tokens = rows * cols
    share = channels // parts
    width = w_query.shape[0]
    positions = parts * tokens
    number = positions * (channels // GROUPS)

    loads = [
        pltpu.make_async_copy(source, target, load_sem.at[index])
        for index, (source, target) in enumerate(
            [(conv_weight, wconv), (w_query, wq), (w_keyvalue, wkv), (w_out, wo)]
        )
    ]
    for load in loads:
        load.start()

    barrier = pltpu.get_barrier_semaphore()
    for distance in range(1, parts):
        pl.semaphore_signal(
            barrier,
            inc=1,
            device_id={"patch": lax.rem(me + distance, parts)},
            device_id_type=MESH,
        )

    def gather(block_of, sems, i):
        return Gather(parts, me, block_of.at[i, me], block_of.at[i], *[sems.at[i, k] for k in range(4)])

    acts = [
        Gather(parts, me, act.at[0, me], act.at[0], *[act_sem.at[k] for k in range(4)])
    ]
    stats = [gather(stat, stat_sem, step) for step in range(STEPS)]
    cens = [gather(cen, cen_sem, step) for step in range(STEPS)]
    kvs = [
        Gather(parts, me, source, kv.at[i], *[kv_sem.at[i, k] for k in range(4)])
        for i, source in enumerate([kv_src] + [kv.at[i, me] for i in range(STEPS - 1)])
    ]

    def exchange(kind, step, source, target, shared=False):
        return Exchange(
            parts, me, source, target, x_send.at[kind, step], x_recv.at[kind, step], shared
        )

    norms = [exchange(0, s, nrm_src.at[s], nrm.at[s]) for s in range(STEPS)]
    hiddens = [exchange(1, s, hid_src.at[s], hid.at[s]) for s in range(STEPS)]

    def block(values, index):
        return values[:, index * share : (index + 1) * share]

    def own_share(values):
        picked = jnp.zeros((values.shape[0], share), F32)
        for index in range(parts):
            picked = jnp.where(me == index, block(values, index), picked)
        return picked

    def send_state(step, state):
        sums = moments(state)
        stat[step, me] = sums
        if step > 0:
            stats[step].start()
        cen[step, me] = (state - sums[0:1] * (1.0 / tokens)).astype(BF16)
        if step > 0:
            cens[step].start()

    state = field[...].reshape(tokens, channels)
    send_state(0, state)
    act[0, me] = stale_conv[...].reshape(tokens, channels)
    kv_src[...] = jnp.concatenate(
        [stale_keys[...].astype(F32), stale_values[...].astype(F32)], axis=1
    ).astype(BF16)

    pl.semaphore_wait(barrier, parts - 1)
    for started in (stats[0], cens[0], acts[0]):
        started.start()

    row_shifts = conv_bias[...][None, :] + time_embed[...]
    shifts = own_share(row_shifts)
    gain = own_share(gain2[...][None, :])
    bias = own_share(bias2[...][None, :])
    loads[0].wait()
    for load in loads[1:]:
        load.wait()

    pick = jnp.where(
        lax.broadcasted_iota(jnp.int32, (channels, share), 0) - me * share
        == lax.broadcasted_iota(jnp.int32, (channels, share), 1),
        1.0,
        0.0,
    ).astype(BF16)
    column = lax.broadcasted_iota(jnp.int32, (positions, share), 0) % cols
    head_row = lax.broadcasted_iota(jnp.int32, (HEADS * tokens, width), 0) // tokens
    head_col = lax.broadcasted_iota(jnp.int32, (HEADS * tokens, width), 1) // HEAD_DIM
    on_head = head_row == head_col

    for step in range(STEPS):
        stats[step].forward()
        stats[step].arrive()
        sums = exact_dot(jnp.sum(stat[step], axis=0), to_group[...])
        average, scale = mean_and_scale(sums, number)
        spread = exact_dot(jnp.concatenate([average, scale], axis=0), from_group[...])
        slope = spread[1:2] * gain1[...][None, :]
        average = spread[0:1]

        def activate(which):
            mean = stat[step, which][0:1] * (1.0 / tokens)
            offset = (mean - average) * slope + bias1[...][None, :]
            value = cen[step, which].astype(F32) * slope + offset
            act[step + 1, which] = (value * jax.nn.sigmoid(value)).astype(BF16)

        cens[step].walk(activate)
        means = stat[step][:, 0, :] * (1.0 / tokens)
        held = jnp.dot(
            cen[step].reshape(positions, channels), pick, preferred_element_type=F32
        ).reshape(parts, tokens, share) + exact_dot(means, pick)[:, None, :]
        if step == 0:
            kvs[0].start()
            acts[0].forward()
            acts[0].arrive()

        def piece(which, row):
            return act[which, row // rows, (row % rows) * cols : (row % rows + 1) * cols, :]

        whole = parts * rows
        nothing = jnp.zeros((cols, channels), BF16)
        conv = None
        for tap in range(3):
            pieces = []
            for row in range(whole):
                near = row + tap - 1
                if near < 0 or near >= whole:
                    pieces.append(nothing)
                else:
                    same = near // rows == row // rows
                    pieces.append(piece(step + 1 if same else step, near))
            term = dot_transposed(
                jnp.concatenate(pieces, axis=0), wconv[tap].reshape(3 * share, channels)
            )
            conv = term if conv is None else conv + term
        before = pltpu.roll(block(conv, 0), 1, 0)
        after = pltpu.roll(block(conv, 2), positions - 1, 0)
        conv = (
            block(conv, 1)
            + jnp.where(column == 0, 0.0, before)
            + jnp.where(column == cols - 1, 0.0, after)
        )
        hidden = held.reshape(positions, share) + (conv + shifts[step : step + 1])
        average, scale = mean_and_scale(exact_dot(moments(hidden), same_group[...]), number)
        normed = ((hidden - average) * scale * gain + bias).astype(BF16)
        nrm_src[step] = normed.reshape(parts, tokens, share)
        norms[step].start()
        hid_src[step] = conv.astype(BF16).reshape(parts, tokens, share)
        hiddens[step].start()
        nrm[step, me] = nrm_src[step, me]
        hid[step, me] = hid_src[step, me]
        if step == 0:
            kvs[0].forward()
        norms[step].arrive()
        mine = jnp.concatenate(
            [nrm[step, index].astype(F32) for index in range(parts)], axis=1
        ).astype(BF16)
        fresh = jnp.dot(mine, wkv[...], preferred_element_type=F32).astype(BF16)
        kv[step, me] = fresh
        if step + 1 < STEPS:
            kvs[step + 1].start()
        query = dot_transposed(mine, wq[...]).astype(BF16)
        query = jnp.concatenate([query] * HEADS, axis=0)
        query = jnp.where(on_head, query.astype(F32), 0.0).astype(BF16)
        if step > 0:
            kvs[step].forward()
        kvs[step].arrive()
        both = kv[step].reshape(positions, 2 * width)
        scores = dot_transposed(query, both[:, :width]) * HEAD_DIM ** (-0.5)
        expo = jnp.exp(scores - jnp.max(scores, axis=-1, keepdims=True))
        totals = jnp.sum(expo, axis=-1, keepdims=True)
        summed = jnp.dot(expo.astype(BF16), both, preferred_element_type=F32)[:, width:]
        summed = jnp.where(on_head, summed / totals, 0.0)
        attended = jnp.sum(summed.reshape(HEADS, tokens, width), axis=0).astype(BF16)
        mixed = jnp.dot(attended, wo[...], preferred_element_type=F32)
        hiddens[step].arrive()
        convolved = jnp.concatenate(
            [hid[step, index].astype(F32) for index in range(parts)], axis=1
        )
        state = (state + (convolved + row_shifts[step : step + 1])) + mixed
        if step + 1 < STEPS:
            send_state(step + 1, state)
        out[step] = state.reshape(rows, cols, channels)

    for started in acts + kvs + stats + cens + norms + hiddens:
        started.drain()


def per_device(
    field,
    stale_conv_in,
    stale_keys,
    stale_values,
    norm1_gain,
    norm1_bias,
    conv_weight,
    conv_bias,
    time_embed,
    norm2_gain,
    norm2_bias,
    w_query,
    w_keyvalue,
    w_out,
):
    parts = lax.axis_size("patch")
    rows, cols, channels = field.shape
    tokens = rows * cols
    share = channels // parts
    width = w_query.shape[1]
    members = channels // GROUPS
    chips = parts // CORES
    group_of = np.arange(channels) // members
    to_group = (group_of[:, None] == np.arange(LANES)[None, :]).astype(np.float32)
    same_group = (group_of[:share, None] == group_of[None, :share]).astype(np.float32)
    vmem = pl.BlockSpec(memory_space=pltpu.VMEM)
    away = pl.BlockSpec(memory_space=pl.ANY)
    dma = pltpu.SemaphoreType.DMA
    return pl.pallas_call(
        functools.partial(kernel, parts),
        out_shape=jax.ShapeDtypeStruct((STEPS, rows, cols, channels), F32),
        in_specs=[vmem] * 6 + [away] + [vmem] * 4 + [away] * 3 + [vmem] * 3,
        out_specs=vmem,
        scratch_shapes=[
            pltpu.VMEM((3, 3, share, channels), BF16),
            pltpu.VMEM((width, channels), BF16),
            pltpu.VMEM(w_keyvalue.shape, BF16),
            pltpu.VMEM(w_out.shape, BF16),
            pltpu.VMEM((STEPS + 1, parts, tokens, channels), BF16),
            pltpu.VMEM((tokens, 2 * width), BF16),
            pltpu.VMEM((STEPS, parts, tokens, 2 * width), BF16),
            pltpu.VMEM((STEPS, parts, 2, channels), F32),
            pltpu.VMEM((STEPS, parts, tokens, channels), BF16),
            pltpu.VMEM((STEPS, parts, tokens, share), BF16),
            pltpu.VMEM((STEPS, parts, tokens, share), BF16),
            pltpu.VMEM((STEPS, parts, tokens, share), BF16),
            pltpu.VMEM((STEPS, parts, tokens, share), BF16),
            dma((4,)),
            dma((4, chips)),
            dma((STEPS, 4, chips)),
            dma((STEPS, 4, chips)),
            dma((STEPS, 4, chips)),
            dma((2, STEPS, parts)),
            dma((2, STEPS, parts)),
        ],
        compiler_params=pltpu.CompilerParams(
            collective_id=0, has_side_effects=True, vmem_limit_bytes=56 * 1024 * 1024
        ),
        cost_estimate=pl.CostEstimate(
            flops=2 * STEPS * parts * tokens * 9 * channels * share,
            bytes_accessed=2 * (9 * channels * share + 2 * channels * channels),
            transcendentals=0,
        ),
    )(
        field,
        stale_conv_in,
        stale_keys,
        stale_values,
        norm1_gain,
        norm1_bias,
        conv_weight.transpose(0, 1, 3, 2),
        conv_bias,
        time_embed,
        norm2_gain,
        norm2_bias,
        w_query.T,
        w_keyvalue,
        w_out,
        jnp.asarray(to_group, BF16),
        jnp.asarray(to_group.T, BF16),
        jnp.asarray(same_group, BF16),
    )


def solution(mesh):
    spread = ("req", "patch")
    return jax.shard_map(
        per_device,
        mesh=mesh,
        in_specs=(
            P(spread, None, None),
            P(spread, None, None),
            P(spread, None),
            P(spread, None),
            P(),
            P(),
            P(None, None, None, "patch"),
            P(),
            P("req", None),
            P(),
            P(),
            P(),
            P(),
            P(),
        ),
        out_specs=P(None, spread, None, None),
        check_vma=False,
    )
```
